32 devices in a mesh: grp: 2 (over x), seq: 8 (over z, y), dp: 2 (over core).
Axes of the slice: x: 2, y: 2, z: 4, core: 2. Of those that a mesh axis runs over, the one named last changes fastest.
Arguments:
- dec_query: bfloat16 [4, 1024, 2048], P(('grp', 'dp'), 'seq'), parts along dimension 0, may hold values from -9 to 9
- enc_key: bfloat16 [4, 4096, 2048], P(('grp', 'dp'), 'seq'), parts along dimension 0, may hold values from -4 to 4
- enc_value: bfloat16 [4, 4096, 2048], P(('grp', 'dp'), 'seq'), parts along dimension 0, may hold values from -6 to 6
- saved_out: bfloat16 [4, 1024, 2048], P(('grp', 'dp'), 'seq'), parts along dimension 0, may hold values from -3 to 3
- d_out: bfloat16 [4, 1024, 2048], P(('grp', 'dp'), 'seq'), parts along dimension 0, may hold values from -24 to 24
- dec_start: int32 [4, 33], P(('grp', 'dp')), parts along dimension 0, may hold values from 0 to 1024, as said below
- enc_start: int32 [4, 33], P(('grp', 'dp')), parts along dimension 0, may hold values from 0 to 4096, as said below
Outputs:
- d_query: bfloat16 [4, 1024, 2048], P(('grp', 'dp'), 'seq'), parts along dimension 0
- d_key: bfloat16 [4, 4096, 2048], P(('grp', 'dp'), 'seq'), parts along dimension 0
- d_value: bfloat16 [4, 4096, 2048], P(('grp', 'dp'), 'seq'), parts along dimension 0
The draws below stay inside these ranges and needn't reach their ends.
There are 2 independent parts, one for each index of `grp`. The reference program is written for one: setup_inputs(seed, part) draws one part's arguments, and reference() takes and returns one part's arrays. A program takes and returns all parts, laid end to end along the dimension named above; each array names one. Nothing has to cross between parts.
Inputs may be any that keep to these rules, and one draw needn't show every extreme that they name: dec_start[b, 0] = 0 and dec_start[b, 32] = 1024; dec_start[b, k] = k * 32 plus a whole number from 0 to 16, so an example has 16 to 48 decoder tokens, and in every batch one example has exactly 48. enc_start[b, 0] = 0 and enc_start[b, 32] = 4096; enc_start[b, k] = k * 4 * 32 plus a whole number from 0 to 64, so an example has 64 to 192 encoder tokens, and in every batch one example has exactly 192.
All inputs are finite; a program needn't handle non-finite values.
Results may differ from the reference program's by a relative error of at most 0.005.
Values may be sent and summed in bfloat16 or wider, within the bound.
A program may use at most 128 MiB of HBM per device.

```python
import jax
import jax.numpy as jnp
from jax import lax

H = 32
HD = 64
Q_DEV = 128
RATIO = 4
G = 32
HK = 2048
E_DEV = 512
Q_TOK = 1024
E_TOK = 4096
NEX = 32
BATCHES = 2
REACH = 128
N_SEQ = 8


def offsets_for(base_key, salt_num, step_rows):
    folded = jax.random.fold_in(base_key, salt_num)
    first_key, second_key = jax.random.split(folded)
    jitter = jax.random.randint(first_key, (BATCHES, NEX + 1), 0, step_rows // 2 + 1)
    forced = jax.random.randint(second_key, (BATCHES, 1), 0, NEX - 1)
    places = jnp.arange(NEX + 1, dtype=jnp.int32)[None, :]
    jitter = jnp.where(places == forced, 0, jitter)
    jitter = jnp.where(places == forced + 1, step_rows // 2, jitter)
    jitter = jnp.where((places == 0) | (places == NEX), 0, jitter)
    return (places * step_rows + jitter).astype(jnp.int32)


def key_values(base_key):
    folded = jax.random.fold_in(base_key, 31)
    values = jax.random.truncated_normal(folded, -4.0, 4.0, (BATCHES, E_TOK, HK), jnp.float32)
    return values


def draw_enc_key(key, part):
    return key_values(key).astype(jnp.bfloat16)


def draw_dec_query(key, part):
    folded = jax.random.fold_in(key, 41)
    values = 0.125 * jax.random.truncated_normal(folded, -4.0, 4.0, (BATCHES, Q_TOK, HK), jnp.float32)
    return values.astype(jnp.bfloat16)


def draw_dec_start(key, part):
    return offsets_for(key, 11, G)


def draw_enc_start(key, part):
    return offsets_for(key, 12, RATIO * G)


def level_of(key, dims, cuts, low, high):
    factor_of = 1.0
    for position, parts in cuts:
        steps = jax.random.uniform(jax.random.fold_in(jax.random.fold_in(key, 6), position), (parts,), jnp.float32, low / len(cuts), high / len(cuts))
        factor_of = factor_of * jnp.repeat(jnp.exp(steps), dims[position] // parts).reshape((-1,) + (1,) * (len(dims) - 1 - position))
    return factor_of


def bell_draw(own_key, dims, deviation, most, pieces=(), kind=jnp.bfloat16):
    drawn = deviation * jax.random.normal(own_key, dims, jnp.float32)
    if pieces:
        drawn = drawn * level_of(own_key, dims, pieces, -0.22, 0.18)
    return jnp.clip(drawn, -most, most).astype(kind)


def setup_inputs(seed: int = 0, part: int = 0) -> dict:
    splits = jax.random.split(jax.random.key(seed), 8)
    own_keys = jax.random.split(jax.random.fold_in(splits[7], part), 8)
    return {
        "dec_query": draw_dec_query(jax.random.fold_in(jax.random.fold_in(splits[7], part), 71), part),
        "enc_key": draw_enc_key(jax.random.fold_in(jax.random.fold_in(splits[7], part), 71), part),
        "enc_value": bell_draw(own_keys[2], (BATCHES, E_TOK, HK), 1.0, 6.0, ((0, 2), (1, 8))),
        "saved_out": bell_draw(own_keys[3], (BATCHES, Q_TOK, HK), 0.5, 3.0, ((0, 2), (1, 8))),
        "d_out": bell_draw(own_keys[4], (BATCHES, Q_TOK, HK), 4.0, 24.0, ((0, 2), (1, 8))),
        "dec_start": draw_dec_start(jax.random.fold_in(jax.random.fold_in(splits[7], part), 71), part),
        "enc_start": draw_enc_start(jax.random.fold_in(jax.random.fold_in(splits[7], part), 71), part),
    }


masked_low = -1e30


def example_ids(positions, starts, total):
    counts = jnp.sum((positions[:, None] >= starts[None, 1:-1]).astype(jnp.int32), axis=1)
    inside = (positions >= 0) & (positions < total)
    return jnp.where(inside, counts, -1).astype(jnp.int32)


def round_low(values):
    low_copy = values.astype(jnp.bfloat16)
    low_copy = lax.optimization_barrier(low_copy)
    return low_copy.astype(jnp.float32)


def window_grads(queries, keys_win, values_win, outputs, grads_out, query_ids, key_ids):
    query_f = queries.astype(jnp.float32)
    key_f = keys_win.astype(jnp.float32)
    value_f = values_win.astype(jnp.float32)
    grad_f = grads_out.astype(jnp.float32)
    output_f = outputs.astype(jnp.float32)
    scores = jnp.einsum("qhd,khd->hqk", query_f, key_f)
    allowed = (query_ids[:, None] == key_ids[None, :])[None]
    masked = jnp.where(allowed, scores, masked_low)
    row_max = jnp.max(masked, axis=2, keepdims=True)
    summed = jnp.sum(jnp.where(allowed, jnp.exp(masked - row_max), 0.0), axis=2, keepdims=True)
    log_total = row_max + jnp.log(summed)
    weights = jnp.where(allowed, jnp.exp(masked - log_total), 0.0)
    weights_low = round_low(weights)
    out_dot = jnp.sum(grad_f * output_f, axis=2).T[:, :, None]
    d_probs = jnp.einsum("qhd,khd->hqk", grad_f, value_f)
    d_scores = round_low(weights * (d_probs - out_dot))
    grad_query = jnp.einsum("hqk,khd->qhd", d_scores, key_f)
    grad_key = jnp.einsum("hqk,qhd->khd", d_scores, query_f)
    grad_value = jnp.einsum("hqk,qhd->khd", weights_low, grad_f)
    return grad_query, grad_key, grad_value


def reference(dec_query, enc_key, enc_value, saved_out, d_out, dec_start, enc_start):
    rim_rows = REACH
    window_rows = E_DEV + 2 * rim_rows
    query_list = []
    key_list = []
    value_list = []
    for batch_idx in range(BATCHES):
        key_pos = jnp.arange(E_TOK + 2 * rim_rows, dtype=jnp.int32) - rim_rows
        key_ids = example_ids(key_pos, enc_start[batch_idx], E_TOK)
        query_ids = example_ids(jnp.arange(Q_TOK, dtype=jnp.int32), dec_start[batch_idx], Q_TOK)
        keys_pad = jnp.pad(enc_key[batch_idx], ((rim_rows, rim_rows), (0, 0)))
        values_pad = jnp.pad(enc_value[batch_idx], ((rim_rows, rim_rows), (0, 0)))
        queries_all = dec_query[batch_idx]
        outputs_all = saved_out[batch_idx]
        grads_all = d_out[batch_idx]

        def shard_step(running, shard_idx):
            key_acc, value_acc = running
            q_start = (shard_idx * Q_DEV).astype(jnp.int32)
            k_start = (shard_idx * E_DEV).astype(jnp.int32)
            queries = lax.dynamic_slice_in_dim(queries_all, q_start, Q_DEV, 0).reshape(Q_DEV, H, HD)
            outputs = lax.dynamic_slice_in_dim(outputs_all, q_start, Q_DEV, 0).reshape(Q_DEV, H, HD)
            grads_out = lax.dynamic_slice_in_dim(grads_all, q_start, Q_DEV, 0).reshape(Q_DEV, H, HD)
            keys_win = lax.dynamic_slice_in_dim(keys_pad, k_start, window_rows, 0).reshape(window_rows, H, HD)
            values_win = lax.dynamic_slice_in_dim(values_pad, k_start, window_rows, 0).reshape(window_rows, H, HD)
            q_ids = lax.dynamic_slice_in_dim(query_ids, q_start, Q_DEV, 0)
            k_ids = lax.dynamic_slice_in_dim(key_ids, k_start, window_rows, 0)
            grad_query, grad_key, grad_value = window_grads(queries, keys_win, values_win, outputs, grads_out, q_ids, k_ids)
            old_key = lax.dynamic_slice_in_dim(key_acc, k_start, window_rows, 0)
            key_acc = lax.dynamic_update_slice_in_dim(key_acc, old_key + grad_key.reshape(window_rows, HK), k_start, 0)
            old_value = lax.dynamic_slice_in_dim(value_acc, k_start, window_rows, 0)
            value_acc = lax.dynamic_update_slice_in_dim(value_acc, old_value + grad_value.reshape(window_rows, HK), k_start, 0)
            return (key_acc, value_acc), grad_query.reshape(Q_DEV, HK).astype(jnp.bfloat16)

        start_acc = jnp.zeros((E_TOK + 2 * rim_rows, HK), jnp.float32)
        (key_acc, value_acc), query_rows = lax.scan(shard_step, (start_acc, start_acc), jnp.arange(N_SEQ, dtype=jnp.int32))
        query_list.append(query_rows.reshape(Q_TOK, HK))
        key_list.append(key_acc[rim_rows:rim_rows + E_TOK].astype(jnp.bfloat16))
        value_list.append(value_acc[rim_rows:rim_rows + E_TOK].astype(jnp.bfloat16))
    return (jnp.stack(query_list), jnp.stack(key_list), jnp.stack(value_list))
```

```python
import functools

import jax
import jax.numpy as jnp
from jax import lax
from jax.experimental import pallas as pl
from jax.experimental.pallas import tpu as pltpu
from jax.sharding import PartitionSpec as P

HD = 64
WIDTH = 256
HPG = WIDTH // HD

masked_low = -1e30
NT = (((1,), (1,)), ((), ()))
TN = (((0,), (0,)), ((), ()))
NN = (((1,), (0,)), ((), ()))


def dot(a, b, dims):
    return lax.dot_general(a, b, dims, preferred_element_type=jnp.float32)


def kernel(
    n_seq, n_loc, step, enc_step,
    ds_ref, es_ref, q_hbm, k_hbm, v_hbm, so_hbm, do_hbm,
    dq_hbm, dk_hbm, dv_hbm,
    q, do, so, k, v, xq, xo, bdq, bdo, sbuf, dsb, psb, kid, st, rst_l, rst_r,
    dq, dqx, rdq_a, rdq_b, dqo, dk, dv,
    in_sem, snd, rcv, out_sem,
):
    me = lax.axis_index("seq")
    has_left = me > 0
    has_right = me < n_seq - 1
    q_rows = n_loc * step
    k_rows = n_loc * enc_step
    half = step // 2
    ehalf = enc_step // 2
    lanes = HPG * step
    groups = q.shape[1] // WIDTH
    last = n_loc + 1

    loads = [
        pltpu.make_async_copy(a.at[0], b, in_sem.at[n])
        for n, (a, b) in enumerate(((q_hbm, q), (k_hbm, k), (v_hbm, v), (do_hbm, do), (so_hbm, so)))
    ]
    for c in loads:
        c.start()

    xq[...] = jnp.zeros_like(xq)
    xo[...] = jnp.zeros_like(xo)
    for r in (rst_l, rst_r):
        r[...] = jnp.zeros_like(r)
        for n in range(2):
            r[n, 0] = jnp.full(r.shape[2:], masked_low, jnp.float32)
    rdq_a[...] = jnp.zeros_like(rdq_a)
    rdq_b[...] = jnp.zeros_like(rdq_b)

    barrier = pltpu.get_barrier_semaphore()

    def signal(to):
        pl.semaphore_signal(
            barrier, inc=1, device_id={"seq": to}, device_id_type=pl.DeviceIdType.MESH
        )

    pl.when(has_left)(lambda: signal(me - 1))
    pl.when(has_right)(lambda: signal(me + 1))
    pl.semaphore_wait(barrier, has_left.astype(jnp.int32) + has_right.astype(jnp.int32))

    def remote(src, dst, n, to):
        return pltpu.make_async_remote_copy(
            src_ref=src, dst_ref=dst, send_sem=snd.at[n], recv_sem=rcv.at[n],
            device_id={"seq": to}, device_id_type=pl.DeviceIdType.MESH,
        )

    tail = pl.ds(q_rows - step, step)
    head = pl.ds(0, half)
    to_right = [
        remote(q_hbm.at[0, tail], xq.at[pl.ds(0, step)], 0, me + 1),
        remote(do_hbm.at[0, tail], xo.at[pl.ds(0, step)], 1, me + 1),
        remote(st.at[pl.ds(last - 1, 2)], rst_l, 2, me + 1),
        remote(dqx.at[pl.ds(step, half)], rdq_a, 3, me + 1),
    ]
    to_left = [
        remote(q_hbm.at[0, head], xq.at[pl.ds(step, half)], 4, me - 1),
        remote(do_hbm.at[0, head], xo.at[pl.ds(step, half)], 5, me - 1),
        remote(st.at[pl.ds(0, 2)], rst_r, 6, me - 1),
        remote(dqx.at[pl.ds(0, step)], rdq_b, 7, me - 1),
    ]

    def start(ns):
        def right():
            for n in ns:
                to_right[n].start()

        def left():
            for n in ns:
                to_left[n].start()

        pl.when(has_right)(right)
        pl.when(has_left)(left)

    def arrived(ns):
        def from_left():
            for n in ns:
                to_right[n].wait_recv()

        def from_right():
            for n in ns:
                to_left[n].wait_recv()

        pl.when(has_left)(from_left)
        pl.when(has_right)(from_right)

    start((0, 1))

    def ids(pos, starts):
        total = jnp.zeros(pos.shape, jnp.int32)
        for t in range(-1, n_loc + 1):
            total += (pos >= starts[0, jnp.maximum(me * n_loc + t, 0)]).astype(jnp.int32)
        return total

    kid[...] = ids(me * k_rows + lax.broadcasted_iota(jnp.int32, (k_rows, lanes), 0), es_ref)
    lane_row = lax.rem(lax.broadcasted_iota(jnp.int32, (1, lanes), 1), step)
    qid = [ids(me * q_rows + (c - 1) * step + lane_row, ds_ref) for c in range(last + 1)]
    lane_head = lax.div(lax.broadcasted_iota(jnp.int32, (step, WIDTH), 1), HD)

    def spread(x):
        return jnp.concatenate(
            [jnp.where(lane_head == h, x, jnp.zeros_like(x)) for h in range(HPG)], axis=0
        )

    def gather(x):
        total = jnp.zeros((step, WIDTH), jnp.float32)
        for h in range(HPG):
            total = jnp.where(lane_head == h, x[h * step : (h + 1) * step], total)
        return total

    def rows_of(c):
        lo = max(0, (c - 2) * enc_step)
        hi = min(k_rows, c * enc_step + ehalf)
        return lo, hi

    s_at = {}
    at = 0
    for c in (0, 1, last - 1, last):
        s_at[c] = at
        at += rows_of(c)[1] - rows_of(c)[0]

    def cols(g):
        return pl.ds(pl.multiple_of(g * WIDTH, WIDTH), WIDTH)

    def blk(c):
        return pl.ds(c * lanes, lanes)

    def build(g, c, qs, dos):
        bdq[g, blk(c)] = spread(qs)
        bdo[g, blk(c)] = spread(dos)

    ones = jnp.ones((8, WIDTH), jnp.bfloat16)

    def out_dot(dos, sos):
        w = dos.astype(jnp.float32) * sos.astype(jnp.float32)
        hi = w.astype(jnp.bfloat16)
        rest = w - hi.astype(jnp.float32)
        mid = rest.astype(jnp.bfloat16)
        low = (rest - mid.astype(jnp.float32)).astype(jnp.bfloat16)
        total = dot(ones, spread(low), NT) + dot(ones, spread(mid), NT) + dot(ones, spread(hi), NT)
        return total[0:1]

    def scores(g, c):
        lo, hi = rows_of(c)
        s = dot(k[lo:hi, cols(g)], bdq[g, blk(c)], NT)
        s = jnp.where(kid[lo:hi] == qid[c], s, masked_low)
        m = jnp.max(s, axis=0, keepdims=True)
        l = jnp.sum(jnp.exp(s - jnp.maximum(m, 0.5 * masked_low)), axis=0, keepdims=True)
        return s, m, l

    def first_pass(g, c):
        s, m, l = scores(g, c)
        sbuf[g, pl.ds(s_at[c], s.shape[0])] = s
        st[c, 0, pl.ds(g, 1)] = m
        st[c, 1, pl.ds(g, 1)] = l

    def second_pass(g, c, s, total, od):
        lo, hi = rows_of(c)
        p = jnp.exp(s - total)
        dp = dot(v[lo:hi, cols(g)], bdo[g, blk(c)], NT)
        dsc = (p * (dp - od)).astype(jnp.bfloat16)
        psb[g, lo:hi, blk(c)] = p.astype(jnp.bfloat16)
        dsb[g, lo:hi, blk(c)] = dsc
        return gather(dot(dsc, k[lo:hi, cols(g)], TN))

    def own(c):
        return pl.ds((c - 1) * step, step)

    for c in loads:
        c.wait()

    @pl.loop(0, groups)
    def _(g):
        for j in range(n_loc):
            z = jnp.zeros((enc_step - ehalf, lanes), jnp.bfloat16)
            psb[g, pl.ds(j * enc_step + ehalf, enc_step - ehalf), blk(j)] = z
            dsb[g, pl.ds(j * enc_step + ehalf, enc_step - ehalf), blk(j)] = z
        for c in range(1, last):
            dos = do[own(c), cols(g)]
            build(g, c, q[own(c), cols(g)], dos)
            od = out_dot(dos, so[own(c), cols(g)])
            if c in (1, last - 1):
                first_pass(g, c)
                st[c, 2, pl.ds(g, 1)] = od
            else:
                s, m, l = scores(g, c)
                dq[own(c), cols(g)] = second_pass(g, c, s, m + jnp.log(l), od)

    arrived((0, 1))

    @pl.loop(0, groups)
    def _(g):
        for c in (0, last):
            r = pl.ds(0 if c == 0 else step, step)
            build(g, c, xq[r, cols(g)], xo[r, cols(g)])
            first_pass(g, c)
            st[c, 2, pl.ds(g, 1)] = jnp.zeros((1, lanes), jnp.float32)

    start((2,))
    arrived((2,))

    def finish(g, c, other, od_ref):
        row = pl.ds(g, 1)
        m1, m2 = st[c, 0, row], other[0, row]
        l1, l2 = st[c, 1, row], other[1, row]
        m = jnp.maximum(m1, m2)
        l = l1 * jnp.exp(m1 - m) + l2 * jnp.exp(m2 - m)
        total = jnp.where(l > 0.0, m + jnp.log(l), 0.0)
        lo, hi = rows_of(c)
        s = sbuf[g, pl.ds(s_at[c], hi - lo)]
        return second_pass(g, c, s, total, od_ref[2, row])

    @pl.loop(0, groups)
    def _(g):
        dqx[pl.ds(0, step), cols(g)] = finish(
            g, 0, rst_l.at[0], rst_l.at[0]).astype(jnp.bfloat16)
        dqx[pl.ds(step, step), cols(g)] = finish(
            g, last, rst_r.at[1], rst_r.at[1]).astype(jnp.bfloat16)

    start((3,))

    outs = []
    @pl.loop(0, groups)
    def _(g):
        dq[own(1), cols(g)] = finish(g, 1, rst_l.at[1], st.at[1])
        dq[own(last - 1), cols(g)] = finish(g, last - 1, rst_r.at[0], st.at[last - 1])
        for j in range(n_loc):
            rows = pl.ds(j * enc_step, enc_step)
            span = pl.ds(j * lanes, 3 * lanes)
            dk[rows, cols(g)] = dot(dsb[g, rows, span], bdq[g, span], NN).astype(jnp.bfloat16)
            dv[rows, cols(g)] = dot(psb[g, rows, span], bdo[g, span], NN).astype(jnp.bfloat16)
        pltpu.make_async_copy(dk.at[:, cols(g)], dk_hbm.at[0, :, cols(g)], out_sem.at[0, g]).start()
        pltpu.make_async_copy(dv.at[:, cols(g)], dv_hbm.at[0, :, cols(g)], out_sem.at[1, g]).start()

    arrived((3,))
    dq[pl.ds(0, half)] = dq[pl.ds(0, half)] + rdq_a[...].astype(jnp.float32)
    dq[tail] = dq[tail] + rdq_b[...].astype(jnp.float32)
    dqo[...] = dq[...].astype(jnp.bfloat16)
    fin = pltpu.make_async_copy(dqo, dq_hbm.at[0], in_sem.at[0])
    fin.start()

    @pl.loop(0, groups)
    def _(g):
        pltpu.make_async_copy(dk.at[:, cols(g)], dk_hbm.at[0, :, cols(g)], out_sem.at[0, g]).wait()
        pltpu.make_async_copy(dv.at[:, cols(g)], dv_hbm.at[0, :, cols(g)], out_sem.at[1, g]).wait()

    fin.wait()

    def sent_right():
        for c in to_right:
            c.wait_send()

    def sent_left():
        for c in to_left:
            c.wait_send()

    pl.when(has_right)(sent_right)
    pl.when(has_left)(sent_left)


def shards(dec_query, enc_key, enc_value, saved_out, d_out, dec_start, enc_start):
    n_seq = lax.axis_size("seq")
    _, q_rows, width = dec_query.shape
    k_rows = enc_key.shape[1]
    n_loc = (dec_start.shape[1] - 1) // n_seq
    step = q_rows // n_loc
    enc_step = k_rows // n_loc
    half = step // 2
    lanes = HPG * step
    groups = width // WIDTH
    chunks = n_loc + 2
    ehalf = enc_step // 2
    held = ehalf + (enc_step + ehalf) + 2 * enc_step + enc_step
    bf, f32 = jnp.bfloat16, jnp.float32
    vm = pltpu.VMEM
    hbm = pl.BlockSpec(memory_space=pl.ANY)
    smem = pl.BlockSpec(memory_space=pltpu.SMEM)
    return pl.pallas_call(
        functools.partial(kernel, n_seq, n_loc, step, enc_step),
        out_shape=(
            jax.ShapeDtypeStruct(dec_query.shape, bf),
            jax.ShapeDtypeStruct(enc_key.shape, bf),
            jax.ShapeDtypeStruct(enc_value.shape, bf),
        ),
        in_specs=[smem, smem] + [hbm] * 5,
        out_specs=(hbm, hbm, hbm),
        scratch_shapes=[
            vm((q_rows, width), bf), vm((q_rows, width), bf), vm((q_rows, width), bf),
            vm((k_rows, width), bf), vm((k_rows, width), bf),
            vm((2 * step, width), bf), vm((2 * step, width), bf),
            vm((groups, chunks * lanes, WIDTH), bf), vm((groups, chunks * lanes, WIDTH), bf),
            vm((groups, held, lanes), f32),
            vm((groups, k_rows, chunks * lanes), bf), vm((groups, k_rows, chunks * lanes), bf),
            vm((k_rows, lanes), jnp.int32),
            vm((chunks, 3, groups, lanes), f32),
            vm((2, 3, groups, lanes), f32), vm((2, 3, groups, lanes), f32),
            vm((q_rows, width), f32), vm((2 * step, width), bf),
            vm((half, width), bf), vm((step, width), bf), vm((q_rows, width), bf),
            vm((k_rows, width), bf), vm((k_rows, width), bf),
            pltpu.SemaphoreType.DMA((5,)),
            pltpu.SemaphoreType.DMA((8,)), pltpu.SemaphoreType.DMA((8,)),
            pltpu.SemaphoreType.DMA((2, groups)),
        ],
        compiler_params=pltpu.CompilerParams(
            collective_id=0, has_side_effects=True, vmem_limit_bytes=56 * 1024 * 1024
        ),
    )(dec_start, enc_start, dec_query, enc_key, enc_value, saved_out, d_out)


def solution(mesh):
    rows = P(("grp", "dp"), "seq", None)
    starts = P(("grp", "dp"), None)
    return jax.shard_map(
        shards,
        mesh=mesh,
        in_specs=(rows, rows, rows, rows, rows, starts, starts),
        out_specs=(rows, rows, rows),
        check_vma=False,
    )
```

```python
import functools

import jax
import jax.numpy as jnp
from jax import lax
from jax.experimental import pallas as pl
from jax.experimental.pallas import tpu as pltpu
from jax.sharding import PartitionSpec as P

HD = 64
WIDTH = 256
HPG = WIDTH // HD

masked_low = -1e30
NT = (((1,), (1,)), ((), ()))
TN = (((0,), (0,)), ((), ()))
NN = (((1,), (0,)), ((), ()))


def dot(a, b, dims):
    return lax.dot_general(a, b, dims, preferred_element_type=jnp.float32)


def kernel(
    n_seq, n_loc, step, enc_step,
    ds_ref, es_ref, q_hbm, k_hbm, v_hbm, so_hbm, do_hbm,
    dq_out, dk, dv,
    q, do, so, k, v, xq, xo, bdq, bdo, sbuf, dsb, psb, kid, st, rst_l, rst_r,
    dq, dqx, rdq_a, rdq_b,
    in_sem, snd, rcv,
):
    me = lax.axis_index("seq")
    has_left = me > 0
    has_right = me < n_seq - 1
    q_rows = n_loc * step
    k_rows = n_loc * enc_step
    half = step // 2
    ehalf = enc_step // 2
    lanes = HPG * step
    groups = q.shape[1] // WIDTH
    last = n_loc + 1

    loads = [
        pltpu.make_async_copy(a.at[0], b, in_sem.at[n])
        for n, (a, b) in enumerate(((q_hbm, q), (k_hbm, k), (v_hbm, v), (do_hbm, do), (so_hbm, so)))
    ]
    for c in loads:
        c.start()

    xq[...] = jnp.zeros_like(xq)
    xo[...] = jnp.zeros_like(xo)
    for r in (rst_l, rst_r):
        r[...] = jnp.zeros_like(r)
        for n in range(2):
            r[n, 0] = jnp.full(r.shape[2:], masked_low, jnp.float32)
    rdq_a[...] = jnp.zeros_like(rdq_a)
    rdq_b[...] = jnp.zeros_like(rdq_b)

    barrier = pltpu.get_barrier_semaphore()

    def signal(to):
        pl.semaphore_signal(
            barrier, inc=1, device_id={"seq": to}, device_id_type=pl.DeviceIdType.MESH
        )

    pl.when(has_left)(lambda: signal(me - 1))
    pl.when(has_right)(lambda: signal(me + 1))
    pl.semaphore_wait(barrier, has_left.astype(jnp.int32) + has_right.astype(jnp.int32))

    def remote(src, dst, n, to):
        return pltpu.make_async_remote_copy(
            src_ref=src, dst_ref=dst, send_sem=snd.at[n], recv_sem=rcv.at[n],
            device_id={"seq": to}, device_id_type=pl.DeviceIdType.MESH,
        )

    tail = pl.ds(q_rows - step, step)
    head = pl.ds(0, half)
    to_right = [
        remote(q_hbm.at[0, tail], xq.at[pl.ds(0, step)], 0, me + 1),
        remote(do_hbm.at[0, tail], xo.at[pl.ds(0, step)], 1, me + 1),
        remote(st.at[pl.ds(last - 1, 2)], rst_l, 2, me + 1),
        remote(dqx.at[pl.ds(step, half)], rdq_a, 3, me + 1),
    ]
    to_left = [
        remote(q_hbm.at[0, head], xq.at[pl.ds(step, half)], 4, me - 1),
        remote(do_hbm.at[0, head], xo.at[pl.ds(step, half)], 5, me - 1),
        remote(st.at[pl.ds(0, 2)], rst_r, 6, me - 1),
        remote(dqx.at[pl.ds(0, step)], rdq_b, 7, me - 1),
    ]

    def start(ns):
        def right():
            for n in ns:
                to_right[n].start()

        def left():
            for n in ns:
                to_left[n].start()

        pl.when(has_right)(right)
        pl.when(has_left)(left)

    def arrived(ns):
        def from_left():
            for n in ns:
                to_right[n].wait_recv()

        def from_right():
            for n in ns:
                to_left[n].wait_recv()

        pl.when(has_left)(from_left)
        pl.when(has_right)(from_right)

    start((0, 1))

    def ids(pos, starts):
        total = jnp.zeros(pos.shape, jnp.int32)
        for t in range(-1, n_loc + 1):
            total += (pos >= starts[0, jnp.maximum(me * n_loc + t, 0)]).astype(jnp.int32)
        return total

    kid[...] = ids(me * k_rows + lax.broadcasted_iota(jnp.int32, (k_rows, lanes), 0), es_ref)
    lane_row = lax.rem(lax.broadcasted_iota(jnp.int32, (1, lanes), 1), step)
    qid = [ids(me * q_rows + (c - 1) * step + lane_row, ds_ref) for c in range(last + 1)]
    lane_head = lax.div(lax.broadcasted_iota(jnp.int32, (step, WIDTH), 1), HD)

    def spread(x):
        return jnp.concatenate(
            [jnp.where(lane_head == h, x, jnp.zeros_like(x)) for h in range(HPG)], axis=0
        )

    def gather(x):
        total = jnp.zeros((step, WIDTH), jnp.float32)
        for h in range(HPG):
            total = jnp.where(lane_head == h, x[h * step : (h + 1) * step], total)
        return total

    def rows_of(c):
        lo = max(0, (c - 2) * enc_step)
        hi = min(k_rows, c * enc_step + ehalf)
        return lo, hi

    s_at = {}
    at = 0
    for c in (0, 1, last - 1, last):
        s_at[c] = at
        at += rows_of(c)[1] - rows_of(c)[0]

    def cols(g):
        return pl.ds(pl.multiple_of(g * WIDTH, WIDTH), WIDTH)

    def blk(c):
        return pl.ds(c * lanes, lanes)

    sel_at = [lax.broadcasted_iota(jnp.int32, (WIDTH, lanes), n) for n in range(2)]
    pick = (lax.div(sel_at[0], HD) == lax.div(sel_at[1], step)).astype(jnp.bfloat16)
    diag_at = [lax.broadcasted_iota(jnp.int32, (step, lanes), n) for n in range(2)]
    diag = diag_at[0] == lax.rem(diag_at[1], step)

    def out_dot(dos, sos):
        w = dos.astype(jnp.float32) * sos.astype(jnp.float32)
        hi = w.astype(jnp.bfloat16)
        low = (w - hi.astype(jnp.float32)).astype(jnp.bfloat16)
        total = dot(hi, pick, NN) + dot(low, pick, NN)
        return jnp.sum(jnp.where(diag, total, 0.0), axis=0, keepdims=True)

    def build(g, cs, qs, dos):
        bq = [spread(x) for x in qs]
        bo = [spread(x) for x in dos]
        for c, x, y in zip(cs, bq, bo):
            bdq[g, blk(c)] = x
            bdo[g, blk(c)] = y
        return bq, bo

    def part(ref, g, c):
        lo, hi = rows_of(c)
        return ref[lo:hi, cols(g)]

    def masked_scores(g, cs, bq):
        raw = [dot(part(k, g, c), x, NT) for c, x in zip(cs, bq)]
        return [
            jnp.where(kid[rows_of(c)[0] : rows_of(c)[1]] == qid[c], s, masked_low)
            for c, s in zip(cs, raw)
        ]

    def totals(ss):
        ms = [jnp.max(s, axis=0, keepdims=True) for s in ss]
        ls = [
            jnp.sum(jnp.exp(s - jnp.maximum(m, 0.5 * masked_low)), axis=0, keepdims=True)
            for s, m in zip(ss, ms)
        ]
        return ms, ls

    def keep(g, c, s, m, l):
        sbuf[g, pl.ds(s_at[c], s.shape[0])] = s
        st[c, 0, pl.ds(g, 1)] = m
        st[c, 1, pl.ds(g, 1)] = l

    def grads(g, cs, bo, ss, lts, ods):
        dps = [dot(part(v, g, c), x, NT) for c, x in zip(cs, bo)]
        ps = [jnp.exp(s - lt) for s, lt in zip(ss, lts)]
        dss = [(p * (dp - od)).astype(jnp.bfloat16) for p, dp, od in zip(ps, dps, ods)]
        turned = [x.T for x in dss]
        dqs = [dot(x, part(k, g, c), NN) for c, x in zip(cs, turned)]
        for c, p, x in zip(cs, ps, dss):
            lo, hi = rows_of(c)
            psb[g, lo:hi, blk(c)] = p.astype(jnp.bfloat16)
            dsb[g, lo:hi, blk(c)] = x
        return [gather(x) for x in dqs]

    def own(c):
        return pl.ds((c - 1) * step, step)

    for c in loads:
        c.wait()

    @pl.loop(0, groups, unroll=4)
    def _(g):
        for j in range(n_loc):
            z = jnp.zeros((enc_step - ehalf, lanes), jnp.bfloat16)
            psb[g, pl.ds(j * enc_step + ehalf, enc_step - ehalf), blk(j)] = z
            dsb[g, pl.ds(j * enc_step + ehalf, enc_step - ehalf), blk(j)] = z
        cs = list(range(1, last))
        doss = [do[own(c), cols(g)] for c in cs]
        bq, bo = build(g, cs, [q[own(c), cols(g)] for c in cs], doss)
        ss = masked_scores(g, cs, bq)
        ods = [out_dot(x, so[own(c), cols(g)]) for c, x in zip(cs, doss)]
        ms, ls = totals(ss)
        for n in (0, -1):
            keep(g, cs[n], ss[n], ms[n], ls[n])
            st[cs[n], 2, pl.ds(g, 1)] = ods[n]
        inner = cs[1:-1]
        lts = [m + jnp.log(l) for m, l in zip(ms[1:-1], ls[1:-1])]
        for c, x in zip(inner, grads(g, inner, bo[1:-1], ss[1:-1], lts, ods[1:-1])):
            dq[own(c), cols(g)] = x

    arrived((0, 1))

    @pl.loop(0, groups, unroll=4)
    def _(g):
        cs = (0, last)
        both = [pl.ds(0, step), pl.ds(step, step)]
        bq, bo = build(g, cs, [xq[r, cols(g)] for r in both], [xo[r, cols(g)] for r in both])
        ss = masked_scores(g, cs, bq)
        ms, ls = totals(ss)
        for n in range(2):
            keep(g, cs[n], ss[n], ms[n], ls[n])
            st[cs[n], 2, pl.ds(g, 1)] = jnp.zeros((1, lanes), jnp.float32)

    start((2,))
    arrived((2,))

    def finish(g, cs, others, od_refs):
        row = pl.ds(g, 1)
        ss, lts = [], []
        for c, other in zip(cs, others):
            m1, m2 = st[c, 0, row], other[0, row]
            l1, l2 = st[c, 1, row], other[1, row]
            m = jnp.maximum(m1, m2)
            l = l1 * jnp.exp(m1 - m) + l2 * jnp.exp(m2 - m)
            lts.append(jnp.where(l > 0.0, m + jnp.log(l), 0.0))
            lo, hi = rows_of(c)
            ss.append(sbuf[g, pl.ds(s_at[c], hi - lo)])
        bo = [bdo[g, blk(c)] for c in cs]
        return grads(g, cs, bo, ss, lts, [r[2, row] for r in od_refs])

    edges = (rst_l.at[0], rst_r.at[1])

    @pl.loop(0, groups, unroll=4)
    def _(g):
        a, z = finish(g, (0, last), edges, edges)
        dqx[pl.ds(0, step), cols(g)] = a.astype(jnp.bfloat16)
        dqx[pl.ds(step, step), cols(g)] = z.astype(jnp.bfloat16)

    start((3,))

    @pl.loop(0, groups, unroll=4)
    def _(g):
        a, z = finish(
            g, (1, last - 1), (rst_l.at[1], rst_r.at[0]), (st.at[1], st.at[last - 1])
        )
        dq[own(1), cols(g)] = a
        dq[own(last - 1), cols(g)] = z

    @pl.loop(0, groups, unroll=4)
    def _(g):
        for j in range(n_loc):
            rows = pl.ds(j * enc_step, enc_step)
            span = pl.ds(j * lanes, 3 * lanes)
            dk[0, rows, cols(g)] = dot(dsb[g, rows, span], bdq[g, span], NN).astype(jnp.bfloat16)
            dv[0, rows, cols(g)] = dot(psb[g, rows, span], bdo[g, span], NN).astype(jnp.bfloat16)

    arrived((3,))
    dq[pl.ds(0, half)] = dq[pl.ds(0, half)] + rdq_a[...].astype(jnp.float32)
    dq[tail] = dq[tail] + rdq_b[...].astype(jnp.float32)
    dq_out[0] = dq[...].astype(jnp.bfloat16)

    def sent_right():
        for c in to_right:
            c.wait_send()

    def sent_left():
        for c in to_left:
            c.wait_send()

    pl.when(has_right)(sent_right)
    pl.when(has_left)(sent_left)


def shards(dec_query, enc_key, enc_value, saved_out, d_out, dec_start, enc_start):
    n_seq = lax.axis_size("seq")
    _, q_rows, width = dec_query.shape
    k_rows = enc_key.shape[1]
    n_loc = (dec_start.shape[1] - 1) // n_seq
    step = q_rows // n_loc
    enc_step = k_rows // n_loc
    half = step // 2
    lanes = HPG * step
    groups = width // WIDTH
    chunks = n_loc + 2
    ehalf = enc_step // 2
    held = ehalf + (enc_step + ehalf) + 2 * enc_step + enc_step
    bf, f32 = jnp.bfloat16, jnp.float32
    vm = pltpu.VMEM
    hbm = pl.BlockSpec(memory_space=pl.ANY)
    vmem = pl.BlockSpec(memory_space=vm)
    smem = pl.BlockSpec(memory_space=pltpu.SMEM)
    return pl.pallas_call(
        functools.partial(kernel, n_seq, n_loc, step, enc_step),
        out_shape=(
            vm(dec_query.shape, bf),
            vm(enc_key.shape, bf),
            vm(enc_value.shape, bf),
        ),
        in_specs=[smem, smem] + [hbm] * 5,
        out_specs=(vmem, vmem, vmem),
        scratch_shapes=[
            vm((q_rows, width), bf), vm((q_rows, width), bf), vm((q_rows, width), bf),
            vm((k_rows, width), bf), vm((k_rows, width), bf),
            vm((2 * step, width), bf), vm((2 * step, width), bf),
            vm((groups, chunks * lanes, WIDTH), bf), vm((groups, chunks * lanes, WIDTH), bf),
            vm((groups, held, lanes), f32),
            vm((groups, k_rows, chunks * lanes), bf), vm((groups, k_rows, chunks * lanes), bf),
            vm((k_rows, lanes), jnp.int32),
            vm((chunks, 3, groups, lanes), f32),
            vm((2, 3, groups, lanes), f32), vm((2, 3, groups, lanes), f32),
            vm((q_rows, width), f32), vm((2 * step, width), bf),
            vm((half, width), bf), vm((step, width), bf),
            pltpu.SemaphoreType.DMA((5,)),
            pltpu.SemaphoreType.DMA((8,)), pltpu.SemaphoreType.DMA((8,)),
        ],
        compiler_params=pltpu.CompilerParams(
            collective_id=0, has_side_effects=True, vmem_limit_bytes=48 * 1024 * 1024
        ),
    )(dec_start, enc_start, dec_query, enc_key, enc_value, saved_out, d_out)


def solution(mesh):
    rows = P(("grp", "dp"), "seq", None)
    starts = P(("grp", "dp"), None)
    return jax.shard_map(
        shards,
        mesh=mesh,
        in_specs=(rows, rows, rows, rows, rows, starts, starts),
        out_specs=(rows, rows, rows),
        check_vma=False,
    )
```
